256 devices in a mesh: prefix: 32 (over x, y, core), req: 8 (over z).
Axes of the slice: x: 4, y: 4, z: 8, core: 2. Of those that a mesh axis runs over, the one named last changes fastest.
Arguments:
- queries: bfloat16 [512, 8192], P(('prefix', 'req')), may hold values from -32 to 32
- prefix_keys: bfloat16 [131072, 1024], P('prefix', 'req'), may hold values from -15 to 15
- prefix_values: bfloat16 [131072, 1024], P('prefix', 'req'), may hold values from -16 to 16
- suffix_keys: bfloat16 [512, 1024, 1024], P(('prefix', 'req')), may hold values from -4 to 4
- suffix_values: bfloat16 [512, 1024, 1024], P(('prefix', 'req')), may hold values from -16 to 16
- suffix_lengths: int32 [512], P(('prefix', 'req')), may hold values from 256 to 1024, as said below
Outputs:
- attended: float32 [512, 8192], P(('prefix', 'req'))
The draws below stay inside these ranges and needn't reach their ends.
Inputs may be any that keep to these rules, and one draw needn't show every extreme that they name: `suffix_lengths`: some request has exactly 1024 live positions.
All inputs are finite; a program needn't handle non-finite values.
Results may differ from the reference program's by a relative error of at most 0.0045.
Values may be sent and summed in bfloat16 or wider, within the bound.
A program may use at most 128 MiB of HBM per device.

```python
import math
import jax
import jax.numpy as jnp
from jax import lax

HEADS = 64
KVH = 8
HD = 128
S_MAX = 1024
REQUESTS = 512
PREFIX = 131072


def drawn_field(key):
    return jax.random.normal(jax.random.fold_in(key, 11), (PREFIX, KVH * HD), jnp.float32)


def draw_prefix_keys(key, part):
    key_field = jnp.clip(0.5 * drawn_field(key), -15.0, 15.0)
    return key_field.astype(jnp.bfloat16)


def draw_queries(key, part):
    own_key = jax.random.fold_in(key, 2)
    query_noise = jnp.clip(5.0 * jax.random.normal(own_key, (REQUESTS, HEADS, HD), jnp.float32), -32.0, 32.0)
    return query_noise.reshape(REQUESTS, HEADS * HD).astype(jnp.bfloat16)


def draw_suffix_lengths(key, part):
    own_key = jax.random.fold_in(key, 3)
    drawn = jax.random.randint(jax.random.fold_in(own_key, 1), (REQUESTS,), S_MAX // 4, S_MAX + 1)
    longest = jax.random.randint(jax.random.fold_in(own_key, 2), (), 0, REQUESTS)
    return jnp.where(jnp.arange(REQUESTS) == longest, S_MAX, drawn).astype(jnp.int32)


def block_scale(key, dims, shards, low, high):
    def one(position, blocks):
        steps = jax.random.uniform(jax.random.fold_in(jax.random.fold_in(key, 6), position), (blocks,), jnp.float32, low / len(shards), high / len(shards))
        return jnp.repeat(jnp.exp(steps), dims[position] // blocks).reshape((-1,) + (1,) * (len(dims) - position - 1))

    loudness = one(*shards[0])
    for cut in shards[1:]:
        loudness = loudness * one(*cut)
    return loudness


def normal_values(rng, shape, spread, reach, pieces=(), dtype=jnp.bfloat16):
    entries = spread * jax.random.normal(rng, shape, jnp.float32)
    if pieces:
        entries = entries * block_scale(rng, shape, pieces, -0.22, 0.18)
    return jnp.clip(entries, -reach, reach).astype(dtype)


def setup_inputs(seed: int = 0) -> dict:
    key_list = jax.random.split(jax.random.key(seed), 7)
    return {
        "queries": draw_queries(jax.random.fold_in(key_list[6], 71), 0),
        "prefix_keys": draw_prefix_keys(jax.random.fold_in(key_list[6], 71), 0),
        "prefix_values": normal_values(key_list[2], (PREFIX, KVH * HD), 4.0, 16.0, ((0, 32), (1, 8))),
        "suffix_keys": normal_values(key_list[3], (REQUESTS, S_MAX, KVH * HD), 0.7, 4.0, ((0, 256),)),
        "suffix_values": normal_values(key_list[4], (REQUESTS, S_MAX, KVH * HD), 4.0, 16.0, ((0, 256),)),
        "suffix_lengths": draw_suffix_lengths(jax.random.fold_in(key_list[6], 71), 0),
    }


def reference(queries, prefix_keys, prefix_values, suffix_keys, suffix_values, suffix_lengths):
    per_group = HEADS // KVH
    score_scale = 1.0 / math.sqrt(HD)
    group_size = math.gcd(REQUESTS, 4)
    block_count = REQUESTS // group_size
    keys_all = prefix_keys.astype(jnp.float32).reshape(PREFIX, KVH, HD)
    values_all = prefix_values.astype(jnp.float32).reshape(PREFIX, KVH, HD)

    def one_block(items):
        query_rows, own_keys, own_values, lengths = items
        query_heads = query_rows.astype(jnp.float32).reshape(group_size, KVH, per_group, HD)
        suffix_k = own_keys.astype(jnp.float32).reshape(group_size, S_MAX, KVH, HD)
        suffix_v = own_values.astype(jnp.float32).reshape(group_size, S_MAX, KVH, HD)
        prefix_scores = jnp.einsum('bjgd,njd->bjgn', query_heads, keys_all) * score_scale
        suffix_scores = jnp.einsum('bjgd,bsjd->bjgs', query_heads, suffix_k) * score_scale
        in_range = lax.broadcasted_iota(jnp.int32, (group_size, 1, 1, S_MAX), 3) < lengths.astype(jnp.int32)[:, None, None, None]
        suffix_scores = jnp.where(in_range, suffix_scores, -jnp.inf)
        row_top = jnp.maximum(lax.optimization_barrier(jnp.max(prefix_scores, axis=-1)), lax.optimization_barrier(jnp.max(suffix_scores, axis=-1)))
        prefix_weights = jnp.exp(prefix_scores - row_top[..., None])
        suffix_weights = jnp.exp(suffix_scores - row_top[..., None])
        row_total = lax.optimization_barrier(jnp.sum(prefix_weights, axis=-1)) + lax.optimization_barrier(jnp.sum(suffix_weights, axis=-1))
        prefix_rounded = lax.optimization_barrier(prefix_weights.astype(jnp.bfloat16)).astype(jnp.float32)
        suffix_rounded = lax.optimization_barrier(suffix_weights.astype(jnp.bfloat16)).astype(jnp.float32)
        summed = jnp.einsum('bjgn,njd->bjgd', prefix_rounded, values_all)
        summed = summed + jnp.einsum('bjgs,bsjd->bjgd', suffix_rounded, suffix_v)
        result = summed / row_total[..., None]
        return result.reshape(group_size, HEADS * HD).astype(jnp.float32)
    blocks = lax.map(one_block, (queries.reshape(block_count, group_size, HEADS * HD), suffix_keys.reshape(block_count, group_size, S_MAX, KVH * HD), suffix_values.reshape(block_count, group_size, S_MAX, KVH * HD), suffix_lengths.reshape(block_count, group_size)))
    return blocks.reshape(REQUESTS, HEADS * HD)
```

```python
import functools
import math

import jax
import jax.numpy as jnp
from jax import lax
from jax.experimental import pallas as pl
from jax.experimental.pallas import tpu as pltpu
from jax.sharding import PartitionSpec as P

HEADS = 64
KVH = 8
HD = 128
GROUP = HEADS // KVH
SIDE = 4
CHIPS = SIDE * SIDE
ZS = 8
CHUNK = 1024
MESH = pl.DeviceIdType.MESH
F32 = jnp.float32
BF16 = jnp.bfloat16
LOG2_SCALE = math.log2(math.e) / math.sqrt(HD)
LOW = -1e30


def hop(a):
    return jnp.where(a == 0, 2, jnp.where(a == 1, 1, jnp.where(a == 2, 3, 0)))


def kernel(
    q_ref, k_hbm, v_hbm, sk_hbm, sv_hbm, len_ref, out_ref,
    kbuf, vbuf, vt, s0, s1, sk, sv, qf, qz, qt, osend, oland, zsend, zland, sfx_o, sfx_b,
    load_sem, sib_send, sib_recv, z1_send, z1_recv, q_send, q_recv, o_send, o_recv, z2_send, z2_recv,
):
    p = lax.axis_index("prefix")
    z = lax.axis_index("req")
    chip = p // 2
    core = p % 2
    cx = chip // SIDE
    cy = chip % SIDE
    sibling = p + 1 - 2 * core
    keys = k_hbm.shape[0]
    rows = 2 * CHIPS * 8

    def chip_at(t):
        return ((cx + hop(t // SIDE)) % SIDE) * SIDE + (cy + hop(t % SIDE)) % SIDE

    def load(src, dst, i):
        copy = pltpu.make_async_copy(src, dst, load_sem.at[i])
        copy.start()
        return copy

    load_v = load(v_hbm, vbuf, 0)
    load_k = load(k_hbm, kbuf.at[0], 1)
    loads = []
    for r in range(2):
        loads.append((load(sk_hbm.at[r], sk.at[r], 2 + 2 * r), load(sv_hbm.at[r], sv.at[r], 3 + 2 * r)))

    barrier = pltpu.get_barrier_semaphore()
    for d in range(1, ZS):
        pl.semaphore_signal(barrier, inc=1, device_id=(p, (z + d) % ZS), device_id_type=MESH)
    for t in range(CHIPS - 1):
        pl.semaphore_signal(barrier, inc=1, device_id=(2 * chip_at(t) + core, z), device_id_type=MESH)
    pl.semaphore_signal(barrier, inc=1, device_id=(sibling, z), device_id_type=MESH)

    own_q = q_ref[...].astype(F32)
    for g in range(KVH):
        for h in range(GROUP):
            at = (g * GROUP + h) * HD
            for r in range(2):
                qf[g, r, h : h + 1, :] = own_q[r : r + 1, at : at + HD]

    pl.semaphore_wait(barrier, ZS - 1 + CHIPS - 1 + 1)

    def z1_copy(other):
        return pltpu.make_async_remote_copy(
            src_ref=qf.at[other], dst_ref=qz.at[z],
            send_sem=z1_send.at[other], recv_sem=z1_recv.at[z],
            device_id=(p, other), device_id_type=MESH,
        )

    def z1_arrival(other):
        return pltpu.make_async_remote_copy(
            src_ref=qf.at[other], dst_ref=qz.at[other],
            send_sem=z1_send.at[other], recv_sem=z1_recv.at[other],
            device_id=(p, other), device_id_type=MESH,
        )

    for d in range(1, ZS):
        z1_copy((z + d) % ZS).start()
    qz[z] = qf[z]

    sib_k = pltpu.make_async_remote_copy(
        src_ref=k_hbm, dst_ref=kbuf.at[1],
        send_sem=sib_send.at[0], recv_sem=sib_recv.at[0],
        device_id=(sibling, z), device_id_type=MESH,
    )
    sib_k.start()
    load_v.wait()
    for c in range(keys // CHUNK):
        part = vbuf[c * CHUNK : (c + 1) * CHUNK, :].astype(F32)
        vt[0, :, c * CHUNK : (c + 1) * CHUNK] = part.T.astype(BF16)
    sib_v = pltpu.make_async_remote_copy(
        src_ref=vt.at[0], dst_ref=vt.at[1],
        send_sem=sib_send.at[1], recv_sem=sib_recv.at[1],
        device_id=(sibling, z), device_id_type=MESH,
    )
    sib_v.start()

    for d in range(1, ZS):
        z1_arrival((z + d) % ZS).wait_recv()
    qt[chip] = qz[...].reshape(2 * ZS * GROUP, HD).T.astype(BF16)

    def q_copy(t):
        return pltpu.make_async_remote_copy(
            src_ref=qt.at[chip], dst_ref=qt.at[chip],
            send_sem=q_send.at[t], recv_sem=q_recv.at[chip],
            device_id=(2 * chip_at(t) + core, z), device_id_type=MESH,
        )

    def q_arrival(t):
        c = chip_at(t)
        return pltpu.make_async_remote_copy(
            src_ref=qt.at[c], dst_ref=qt.at[c],
            send_sem=q_send.at[t], recv_sem=q_recv.at[c],
            device_id=(2 * c + core, z), device_id_type=MESH,
        )

    for t in range(CHIPS - 1):
        q_copy(t).start()

    for r in range(2):
        loads[r][0].wait()
        loads[r][1].wait()
        live = lax.broadcasted_iota(jnp.int32, (GROUP, sk.shape[1]), 1) < len_ref[r]
        for g in range(KVH):
            q8 = qf[g, r].astype(BF16)
            s = lax.dot_general(
                q8, sk[r, :, g * HD : (g + 1) * HD], (((1,), (1,)), ((), ())),
                preferred_element_type=F32,
            )
            s = jnp.where(live, s * LOG2_SCALE, LOW)
            top = jnp.max(s, axis=1, keepdims=True)
            w = jnp.exp2(s - top)
            total = jnp.sum(w, axis=1, keepdims=True)
            o = jnp.dot(w.astype(BF16), sv[r, :, g * HD : (g + 1) * HD], preferred_element_type=F32)
            sfx_o[g, r] = o / total
            sfx_b[g, r] = jnp.broadcast_to(top + jnp.log2(total), (GROUP, HD))

    load_k.wait()
    sib_k.wait_recv()
    sib_v.wait_recv()
    per_half = keys // CHUNK

    def split_queries(i):
        parts = [qt[chip_at(2 * i + u)] for u in range(2)]
        both = jnp.concatenate(parts, axis=1).astype(F32) * LOG2_SCALE
        high = both.astype(BF16)
        low = (both - high.astype(F32)).astype(BF16)
        return jnp.concatenate([high, low], axis=0)

    def o_copy(t):
        return pltpu.make_async_remote_copy(
            src_ref=osend.at[t], dst_ref=oland.at[chip],
            send_sem=o_send.at[t], recv_sem=o_recv.at[chip],
            device_id=(2 * chip_at(t) + core, z), device_id_type=MESH,
        )

    def o_arrival(t):
        c = chip_at(t)
        return pltpu.make_async_remote_copy(
            src_ref=osend.at[t], dst_ref=oland.at[c],
            send_sem=o_send.at[t], recv_sem=o_recv.at[c],
            device_id=(2 * c + core, z), device_id_type=MESH,
        )

    def step(now, later, i, top):
        if later is not None:
            for u in range(2):
                if not (isinstance(i, int) and 2 * (i + 1) + u == CHIPS - 1):
                    q_arrival(2 * (i + 1) + u).wait_recv()
            queries = split_queries(i + 1)
            new_top = jnp.full((8, rows), LOW, F32)
        if now is not None:
            acc = jnp.zeros((HD, rows), F32)
            total = jnp.zeros((8, rows), F32)
        for c in range(2 * per_half):
            half, at = c // per_half, (c % per_half) * CHUNK
            here = slice(c * CHUNK, (c + 1) * CHUNK)
            if later is not None:
                k = kbuf[half, at : at + CHUNK, :]
                s = jnp.dot(jnp.concatenate([k, k], axis=1), queries, preferred_element_type=F32)
                later[here, :] = s
                new_top = jnp.maximum(new_top, s.reshape(CHUNK // 8, 8, rows).max(axis=0))
            if now is not None:
                w = jnp.exp2(now[here, :] - top)
                total = total + w.reshape(CHUNK // 8, 8, rows).sum(axis=0)
                acc = acc + jnp.dot(vt[half, :, at : at + CHUNK], w.astype(BF16), preferred_element_type=F32)
        if now is not None:
            mass = jnp.broadcast_to(total.sum(axis=0, keepdims=True), (4, rows))
            mass = jnp.concatenate([mass, jnp.broadcast_to(top, (4, rows))], axis=0)
            for u in range(2):
                t = 2 * i + u
                cols = slice(u * rows // 2, (u + 1) * rows // 2)
                osend[t, :HD, :] = acc[:, cols]
                osend[t, HD:, :] = mass[:, cols]
                if not (isinstance(i, int) and t == CHIPS - 1):
                    o_copy(t).start()
        if later is not None:
            return new_top.max(axis=0, keepdims=True)

    pairs = CHIPS // 2
    top = step(None, s0, -1, None)

    def two_steps(j, top):
        top = step(s0, s1, 2 * j, top)
        return step(s1, s0, 2 * j + 1, top)

    top = lax.fori_loop(0, pairs // 2 - 1, two_steps, top)
    top = step(s0, s1, pairs - 2, top)
    step(s1, None, pairs - 1, top)

    for t in range(CHIPS - 1):
        o_arrival(t).wait_recv()
    tops = [oland[chip_at(t), HD + 4 : HD + 5, :] for t in range(CHIPS - 1)]
    tops.append(osend[CHIPS - 1, HD + 4 : HD + 5, :])
    top = functools.reduce(jnp.maximum, tops)
    acc = jnp.zeros((HD, rows // 2), F32)
    total = jnp.zeros((1, rows // 2), F32)
    for t in range(CHIPS):
        part = osend.at[t] if t == CHIPS - 1 else oland.at[chip_at(t)]
        share = jnp.exp2(tops[t] - top)
        acc = acc + part[:HD, :] * share
        total = total + part[HD : HD + 1, :] * share
    zsend[:, 0] = (acc / total).T.reshape(ZS, 2 * GROUP, HD)
    zsend[:, 1] = jnp.broadcast_to(top + jnp.log2(total), (HD, rows // 2)).T.reshape(ZS, 2 * GROUP, HD)

    def z2_copy(other):
        return pltpu.make_async_remote_copy(
            src_ref=zsend.at[other], dst_ref=zland.at[z],
            send_sem=z2_send.at[other], recv_sem=z2_recv.at[z],
            device_id=(p, other), device_id_type=MESH,
        )

    def z2_arrival(other):
        return pltpu.make_async_remote_copy(
            src_ref=zsend.at[other], dst_ref=zland.at[other],
            send_sem=z2_send.at[other], recv_sem=z2_recv.at[other],
            device_id=(p, other), device_id_type=MESH,
        )

    for d in range(1, ZS):
        z2_copy((z + d) % ZS).start()
    zland[z] = zsend[z]
    for d in range(1, ZS):
        z2_arrival((z + d) % ZS).wait_recv()
    for g in range(KVH):
        o = zland[g, 0].reshape(2, GROUP, HD)
        b = zland[g, 1].reshape(2, GROUP, HD)
        share = 1.0 / (1.0 + jnp.exp2(sfx_b[g] - b))
        out_ref[:, g] = o * share + sfx_o[g] * (1.0 - share)

    for d in range(1, ZS):
        z1_copy((z + d) % ZS).wait_send()
        z2_copy((z + d) % ZS).wait_send()
    for t in range(CHIPS - 1):
        q_copy(t).wait_send()
        o_copy(t).wait_send()
    sib_k.wait_send()
    sib_v.wait_send()


def local(queries, prefix_keys, prefix_values, suffix_keys, suffix_values, suffix_lengths):
    keys = prefix_keys.shape[0]
    positions = suffix_keys.shape[1]
    rows = 2 * CHIPS * 8
    dma = pltpu.SemaphoreType.DMA
    hbm = pl.BlockSpec(memory_space=pl.ANY)
    out = pl.pallas_call(
        kernel,
        out_shape=jax.ShapeDtypeStruct((2, KVH, GROUP, HD), F32),
        in_specs=[
            pl.BlockSpec(memory_space=pltpu.VMEM), hbm, hbm, hbm, hbm,
            pl.BlockSpec(memory_space=pltpu.SMEM),
        ],
        out_specs=pl.BlockSpec(memory_space=pltpu.VMEM),
        scratch_shapes=[
            pltpu.VMEM((2, keys, HD), BF16),
            pltpu.VMEM((keys, HD), BF16),
            pltpu.VMEM((2, HD, keys), BF16),
            pltpu.VMEM((2 * keys, rows), F32),
            pltpu.VMEM((2 * keys, rows), F32),
            pltpu.VMEM((2, positions, KVH * HD), BF16),
            pltpu.VMEM((2, positions, KVH * HD), BF16),
            pltpu.VMEM((KVH, 2, GROUP, HD), F32),
            pltpu.VMEM((ZS, 2, GROUP, HD), F32),
            pltpu.VMEM((CHIPS, HD, rows // 2), BF16),
            pltpu.VMEM((CHIPS, HD + 8, rows // 2), F32),
            pltpu.VMEM((CHIPS, HD + 8, rows // 2), F32),
            pltpu.VMEM((ZS, 2, 2 * GROUP, HD), F32),
            pltpu.VMEM((KVH, 2, 2 * GROUP, HD), F32),
            pltpu.VMEM((KVH, 2, GROUP, HD), F32),
            pltpu.VMEM((KVH, 2, GROUP, HD), F32),
            dma((6,)),
            dma((2,)), dma((2,)),
            dma((ZS,)), dma((ZS,)),
            dma((CHIPS,)), dma((CHIPS,)),
            dma((CHIPS,)), dma((CHIPS,)),
            dma((ZS,)), dma((ZS,)),
        ],
        compiler_params=pltpu.CompilerParams(
            collective_id=0, has_side_effects=True, vmem_limit_bytes=56 * 2**20
        ),
        name="attend",
    )(queries, prefix_keys, prefix_values, suffix_keys, suffix_values, suffix_lengths)
    return out.reshape(2, HEADS * HD)


def solution(mesh):
    return jax.shard_map(
        local,
        mesh=mesh,
        in_specs=(
            P(("prefix", "req"), None),
            P("prefix", "req"),
            P("prefix", "req"),
            P(("prefix", "req"), None, None),
            P(("prefix", "req"), None, None),
            P(("prefix", "req")),
        ),
        out_specs=P(("prefix", "req"), None),
        check_vma=False,
    )
```

```python
import functools
import math

import jax
import jax.numpy as jnp
from jax import lax
from jax.experimental import pallas as pl
from jax.experimental.pallas import tpu as pltpu
from jax.sharding import PartitionSpec as P

HEADS = 64
KVH = 8
HD = 128
GROUP = HEADS // KVH
SIDE = 4
CHIPS = SIDE * SIDE
ZS = 8
CHUNK = 1024
MESH = pl.DeviceIdType.MESH
F32 = jnp.float32
BF16 = jnp.bfloat16
LOG2_SCALE = math.log2(math.e) / math.sqrt(HD)
LOW = -1e30
OWNERS = (
    (0, 0), (1, 0), (1, 1), (2, 0), (0, 2), (1, 2), (2, 1), (2, 2),
    (3, 2), (2, 3), (1, 3), (3, 1), (3, 3), (0, 1), (3, 0), (0, 3),
)
STRAIGHT = 3
JOINED = CHIPS - STRAIGHT


def offset(t, axis):
    if isinstance(t, int):
        return OWNERS[t][axis]
    return sum(jnp.where(t == i, o[axis], 0) for i, o in enumerate(OWNERS) if o[axis])


def kernel(
    q_hbm, k_hbm, v_hbm, sk_hbm, sv_hbm, len_hbm, out_ref,
    q_ref, len_ref, kbuf, vbuf, vt, s0, s1, sk, sv, qf, qb, qz, qt, osend, oland,
    jsend, jland, dsend, dland, mcols, sfx_o, sfx_b, own_o, own_m,
    load_sem, sib_send, sib_recv, z1_send, z1_recv, q_send, q_recv, o_send, o_recv, z2_send, z2_recv,
):
    p = lax.axis_index("prefix")
    z = lax.axis_index("req")
    core = p % 2
    cx = p // 2 // SIDE
    cy = p // 2 % SIDE
    sibling = p + 1 - 2 * core
    keys = k_hbm.shape[0]
    own_rows = 2 * ZS * GROUP

    def owner(t):
        return (((cx + offset(t, 0)) % SIDE) * SIDE + (cy + offset(t, 1)) % SIDE) * 2 + core

    def worker(t):
        return (((cx + SIDE - offset(t, 0)) % SIDE) * SIDE + (cy + SIDE - offset(t, 1)) % SIDE) * 2 + core

    barrier = pltpu.get_barrier_semaphore()

    def greet(device):
        pl.semaphore_signal(barrier, inc=1, device_id=device, device_id_type=MESH)

    for d in range(1, ZS):
        greet((p, (z + d) % ZS))
    for t in range(1, CHIPS):
        greet((worker(t), z))
    greet((sibling, z))

    def load(src, dst, i):
        copy = pltpu.make_async_copy(src, dst, load_sem.at[i])
        copy.start()
        return copy

    load_q = load(q_hbm, q_ref, 6)
    load_len = load(len_hbm, len_ref, 7)
    load_v = load(v_hbm, vbuf, 0)
    load_k = load(k_hbm, kbuf.at[0], 1)
    loads = []
    for r in range(2):
        loads.append((load(sk_hbm.at[r], sk.at[r], 2 + 2 * r), load(sv_hbm.at[r], sv.at[r], 3 + 2 * r)))

    load_q.wait()
    own_q = q_ref[...].astype(F32)
    for g in range(KVH):
        for h in range(GROUP):
            at = (g * GROUP + h) * HD
            for r in range(2):
                qf[g, r * GROUP + h : r * GROUP + h + 1, :] = own_q[r : r + 1, at : at + HD]
    for g in range(KVH):
        qb[g] = qf[g].astype(BF16)

    pl.semaphore_wait(barrier, (ZS - 1) + (CHIPS - 1) + 1)

    def z1_copy(d):
        other = (z + d) % ZS
        return pltpu.make_async_remote_copy(
            src_ref=qb.at[other], dst_ref=qz.at[z],
            send_sem=z1_send.at[other], recv_sem=z1_recv.at[z],
            device_id=(p, other), device_id_type=MESH,
        )

    def z1_arrival(d):
        other = (z + d) % ZS
        return pltpu.make_async_remote_copy(
            src_ref=qb.at[other], dst_ref=qz.at[other],
            send_sem=z1_send.at[other], recv_sem=z1_recv.at[other],
            device_id=(p, other), device_id_type=MESH,
        )

    far_first = (4, 3, 5, 2, 6, 1, 7)
    for d in far_first:
        z1_copy(d).start()
    qz[z] = qb[z]

    sib_k = pltpu.make_async_remote_copy(
        src_ref=k_hbm, dst_ref=kbuf.at[1],
        send_sem=sib_send.at[0], recv_sem=sib_recv.at[0],
        device_id=(sibling, z), device_id_type=MESH,
    )
    sib_k.start()
    load_v.wait()
    for c in range(keys // CHUNK):
        part = vbuf[c * CHUNK : (c + 1) * CHUNK, :].astype(F32)
        vt[0, :, c * CHUNK : (c + 1) * CHUNK] = part.T.astype(BF16)
    sib_v = pltpu.make_async_remote_copy(
        src_ref=vt.at[0], dst_ref=vt.at[1],
        send_sem=sib_send.at[1], recv_sem=sib_recv.at[1],
        device_id=(sibling, z), device_id_type=MESH,
    )
    sib_v.start()

    def suffix(r):
        loads[r][0].wait()
        loads[r][1].wait()
        scores = []
        for g in range(KVH):
            q8 = qf[g, r * GROUP : (r + 1) * GROUP, :].astype(BF16)
            scores.append(lax.dot_general(
                q8, sk[r, :, g * HD : (g + 1) * HD], (((1,), (1,)), ((), ())),
                preferred_element_type=F32,
            ))
        s = jnp.concatenate(scores, axis=0)
        live = lax.broadcasted_iota(jnp.int32, s.shape, 1) < len_ref[r]
        s = jnp.where(live, s * LOG2_SCALE, LOW)
        top = jnp.max(s, axis=1, keepdims=True)
        w = jnp.exp2(s - top)
        total = jnp.sum(w, axis=1, keepdims=True)
        mass = jnp.broadcast_to(top + jnp.log2(total), (HEADS, HD))
        share = 1.0 / total
        w = w.astype(BF16)
        for g in range(KVH):
            heads = slice(g * GROUP, (g + 1) * GROUP)
            o = jnp.dot(w[heads], sv[r, :, g * HD : (g + 1) * HD], preferred_element_type=F32)
            sfx_o[g, r * GROUP : (r + 1) * GROUP, :] = o * share[heads]
            sfx_b[g, r * GROUP : (r + 1) * GROUP, :] = mass[heads]

    load_len.wait()
    suffix(0)
    suffix(1)

    for d in far_first:
        z1_arrival(d).wait_recv()
    qt[0] = qz[...].reshape(own_rows, HD).astype(F32).T.astype(BF16)

    def q_copy(t):
        return pltpu.make_async_remote_copy(
            src_ref=qt.at[0], dst_ref=qt.at[t],
            send_sem=q_send.at[t], recv_sem=q_recv.at[t],
            device_id=(worker(t), z), device_id_type=MESH,
        )

    for t in range(1, CHIPS):
        q_copy(t).start()

    load_k.wait()
    sib_k.wait_recv()
    sib_v.wait_recv()
    per_half = keys // CHUNK

    def split_queries(ts):
        both = jnp.concatenate([qt[t] for t in ts], axis=1).astype(F32) * LOG2_SCALE
        high = both.astype(BF16)
        low = (both - high.astype(F32)).astype(BF16)
        return jnp.concatenate([high, low], axis=0)

    def o_copy(t):
        return pltpu.make_async_remote_copy(
            src_ref=osend.at[t], dst_ref=oland.at[t],
            send_sem=o_send.at[t], recv_sem=o_recv.at[t],
            device_id=(owner(t), z), device_id_type=MESH,
        )

    def z2_copy(k, d):
        other = (z + d) % ZS
        return pltpu.make_async_remote_copy(
            src_ref=dsend.at[k - 1, other] if k else jsend.at[other],
            dst_ref=dland.at[k - 1, z] if k else jland.at[z],
            send_sem=z2_send.at[k, other], recv_sem=z2_recv.at[k, z],
            device_id=(owner(JOINED + k - 1) if k else p, other), device_id_type=MESH,
        )

    def z2_arrival(k, d):
        other = (z + d) % ZS
        return pltpu.make_async_remote_copy(
            src_ref=dsend.at[k - 1, other] if k else jsend.at[other],
            dst_ref=dland.at[k - 1, other] if k else jland.at[other],
            send_sem=z2_send.at[k, other], recv_sem=z2_recv.at[k, other],
            device_id=(owner(JOINED + k - 1) if k else p, other), device_id_type=MESH,
        )

    def others(k):
        return far_first + ((0,) if k else ())

    def three(mass):
        first = mass.astype(BF16).astype(F32)
        second = (mass - first).astype(BF16).astype(F32)
        row = lax.broadcasted_iota(jnp.int32, (2 * GROUP, own_rows), 0)
        third = jnp.where(row == 2, mass - first - second, 0.0)
        return jnp.where(row == 0, first, jnp.where(row == 1, second, third)).astype(BF16)

    def mass_of(tile):
        tile = tile.astype(F32)
        return tile[0:1] + tile[1:2] + tile[2:3]

    def send_straight(k, o, mass):
        o = o.T.reshape(ZS, 2 * GROUP, HD).astype(BF16)
        tile = three(mass)
        for other in range(ZS):
            dsend[k - 1, other, : 2 * GROUP, :] = o[other]
            dsend[k - 1, other, 2 * GROUP :, :] = tile
        for d in others(k):
            z2_copy(k, d).start()

    def step(now, later, ts_now, ts_later, top):
        if ts_later:
            cols = len(ts_later) * own_rows
            for t in ts_later:
                if not (isinstance(t, int) and t == 0):
                    q_copy(t).wait_recv()
            queries = split_queries(ts_later)
            new_top = jnp.full((8, cols), LOW, F32)
        if ts_now:
            wide = len(ts_now) * own_rows
            acc = jnp.zeros((HD, wide), F32)
            total = jnp.zeros((8, wide), F32)
        for c in range(2 * per_half):
            half, at = c // per_half, (c % per_half) * CHUNK
            here = slice(c * CHUNK, (c + 1) * CHUNK)
            if ts_later:
                k = kbuf[half, at : at + CHUNK, :]
                s = jnp.dot(jnp.concatenate([k, k], axis=1), queries, preferred_element_type=F32)
                later[here, :cols] = s
                new_top = jnp.maximum(new_top, s.reshape(CHUNK // 8, 8, cols).max(axis=0))
            if ts_now:
                w = jnp.exp2(now[here, :wide] - top)
                total = total + w.reshape(CHUNK // 8, 8, wide).sum(axis=0)
                acc = acc + jnp.dot(vt[half, :, at : at + CHUNK], w.astype(BF16), preferred_element_type=F32)
        if ts_now:
            total = total.sum(axis=0, keepdims=True)
            out = acc * (1.0 / total)
            mass = top + jnp.log2(total)
            for u, t in enumerate(ts_now):
                mine = slice(u * own_rows, (u + 1) * own_rows)
                if isinstance(t, int) and t >= JOINED:
                    send_straight(t - JOINED + 1, out[:, mine], mass[:, mine])
                elif isinstance(t, int) and t == 0:
                    own_o[...] = out
                    own_m[...] = jnp.broadcast_to(mass, (8, own_rows))
                else:
                    osend[t, :HD, :] = out[:, mine].astype(BF16)
                    osend[t, HD:, :] = three(mass[:, mine])
                    o_copy(t).start()
        if ts_later:
            return new_top.max(axis=0, keepdims=True)

    def pair(i):
        return (1 + 2 * i, 2 + 2 * i)

    top = step(None, s0, (), (0,), None)
    step(s0, None, (0,), (), top)
    top = step(None, s0, (), pair(0), None)

    def two_steps(j, top):
        top = step(s0, s1, pair(2 * j), pair(2 * j + 1), top)
        return step(s1, s0, pair(2 * j + 1), pair(2 * j + 2), top)

    rounds = (JOINED - 1) // 4
    top = lax.fori_loop(0, rounds, two_steps, top)
    now, later = s0, s1
    for i in range(2 * rounds, CHIPS // 2 - 1):
        following = pair(i + 1) if i < CHIPS // 2 - 2 else (CHIPS - 1,)
        top = step(now, later, pair(i), following, top)
        now, later = later, now
    step(now, None, (CHIPS - 1,), (), top)

    for t in range(1, JOINED):
        o_copy(t).wait_recv()
    masses = [own_m[0:1, :]] + [mass_of(oland[t, HD:, :]) for t in range(1, JOINED)]
    top = functools.reduce(jnp.maximum, masses)
    shares = [jnp.exp2(mass - top) for mass in masses]
    total = sum(shares)
    out = own_o[...] * shares[0]
    for t in range(1, JOINED):
        out = out + oland[t, :HD, :].astype(F32) * shares[t]
    jsend[:, : 2 * GROUP, :] = (out * (1.0 / total)).T.reshape(ZS, 2 * GROUP, HD)
    jsend[:, 2 * GROUP :, :] = jnp.broadcast_to(top + jnp.log2(total), (ZS, 8, own_rows))
    for d in others(0):
        z2_copy(0, d).start()
    jland[z] = jsend[z]

    kinds = 1 + STRAIGHT
    for k in range(kinds):
        for d in others(k):
            z2_arrival(k, d).wait_recv()
    masses = [jland[g, 2 * GROUP : 2 * GROUP + 1, :] for g in range(KVH)]
    for k in range(STRAIGHT):
        masses += [mass_of(dland[k, g, 2 * GROUP :, :]) for g in range(KVH)]
    mcols[...] = jnp.concatenate(masses, axis=0).T
    mine = mcols[pl.ds(pl.multiple_of(z * 2 * GROUP, 2 * GROUP), 2 * GROUP), :]
    for g in range(KVH):
        masses = [sfx_b[g]]
        for k in range(kinds):
            column = mine[:, k * KVH + g : k * KVH + g + 1]
            masses.append(jnp.broadcast_to(column, (2 * GROUP, HD)))
        outs = [sfx_o[g], jland[g, : 2 * GROUP, :]]
        outs += [dland[k, g, : 2 * GROUP, :].astype(F32) for k in range(STRAIGHT)]
        top = functools.reduce(jnp.maximum, masses)
        shares = [jnp.exp2(m - top) for m in masses]
        joined = sum(o * share for o, share in zip(outs, shares)) / sum(shares)
        for r in range(2):
            for h in range(GROUP):
                at = (g * GROUP + h) * HD
                out_ref[r : r + 1, at : at + HD] = joined[r * GROUP + h : r * GROUP + h + 1, :]

    for d in range(1, ZS):
        z1_copy(d).wait_send()
    for k in range(kinds):
        for d in others(k):
            z2_copy(k, d).wait_send()
    for t in range(1, CHIPS):
        q_copy(t).wait_send()
    for t in range(1, JOINED):
        o_copy(t).wait_send()
    sib_k.wait_send()
    sib_v.wait_send()


def local(queries, prefix_keys, prefix_values, suffix_keys, suffix_values, suffix_lengths):
    keys = prefix_keys.shape[0]
    positions = suffix_keys.shape[1]
    own_rows = 2 * ZS * GROUP
    dma = pltpu.SemaphoreType.DMA
    hbm = pl.BlockSpec(memory_space=pl.ANY)
    return pl.pallas_call(
        kernel,
        out_shape=jax.ShapeDtypeStruct((2, HEADS * HD), F32),
        in_specs=[
            hbm, hbm, hbm, hbm, hbm, hbm,
        ],
        out_specs=pl.BlockSpec(memory_space=pltpu.VMEM),
        scratch_shapes=[
            pltpu.VMEM((2, HEADS * HD), BF16),
            pltpu.SMEM((2,), jnp.int32),
            pltpu.VMEM((2, keys, HD), BF16),
            pltpu.VMEM((keys, HD), BF16),
            pltpu.VMEM((2, HD, keys), BF16),
            pltpu.VMEM((2 * keys, 2 * own_rows), F32),
            pltpu.VMEM((2 * keys, 2 * own_rows), F32),
            pltpu.VMEM((2, positions, KVH * HD), BF16),
            pltpu.VMEM((2, positions, KVH * HD), BF16),
            pltpu.VMEM((KVH, 2 * GROUP, HD), F32),
            pltpu.VMEM((KVH, 2 * GROUP, HD), BF16),
            pltpu.VMEM((ZS, 2 * GROUP, HD), BF16),
            pltpu.VMEM((CHIPS, HD, own_rows), BF16),
            pltpu.VMEM((JOINED, HD + 2 * GROUP, own_rows), BF16),
            pltpu.VMEM((JOINED, HD + 2 * GROUP, own_rows), BF16),
            pltpu.VMEM((ZS, 2 * GROUP + 8, HD), F32),
            pltpu.VMEM((KVH, 2 * GROUP + 8, HD), F32),
            pltpu.VMEM((STRAIGHT, ZS, 4 * GROUP, HD), BF16),
            pltpu.VMEM((STRAIGHT, KVH, 4 * GROUP, HD), BF16),
            pltpu.VMEM((own_rows, (1 + STRAIGHT) * KVH), F32),
            pltpu.VMEM((KVH, 2 * GROUP, HD), F32),
            pltpu.VMEM((KVH, 2 * GROUP, HD), F32),
            pltpu.VMEM((HD, own_rows), F32),
            pltpu.VMEM((8, own_rows), F32),
            dma((8,)),
            dma((2,)), dma((2,)),
            dma((ZS,)), dma((ZS,)),
            dma((CHIPS,)), dma((CHIPS,)),
            dma((JOINED,)), dma((JOINED,)),
            dma((1 + STRAIGHT, ZS)), dma((1 + STRAIGHT, ZS)),
        ],
        compiler_params=pltpu.CompilerParams(
            collective_id=0, has_side_effects=True, vmem_limit_bytes=56 * 2**20
        ),
        name="attend",
    )(queries, prefix_keys, prefix_values, suffix_keys, suffix_values, suffix_lengths)


def solution(mesh):
    return jax.shard_map(
        local,
        mesh=mesh,
        in_specs=(
            P(("prefix", "req"), None),
            P("prefix", "req"),
            P("prefix", "req"),
            P(("prefix", "req"), None, None),
            P(("prefix", "req"), None, None),
            P(("prefix", "req")),
        ),
        out_specs=P(("prefix", "req"), None),
        check_vma=False,
    )
```

```python
import functools
import math

import jax
import jax.numpy as jnp
from jax import lax
from jax.experimental import pallas as pl
from jax.experimental.pallas import tpu as pltpu
from jax.sharding import PartitionSpec as P

HEADS = 64
KVH = 8
HD = 128
GROUP = HEADS // KVH
SIDE = 4
CHIPS = SIDE * SIDE
ZS = 8
CHUNK = 1024
MESH = pl.DeviceIdType.MESH
F32 = jnp.float32
BF16 = jnp.bfloat16
LOG2_SCALE = math.log2(math.e) / math.sqrt(HD)
LOW = -1e30
OWNERS = (
    (0, 0), (1, 0), (0, 1), (2, 0), (0, 2), (3, 1), (1, 2), (2, 1),
    (2, 2), (2, 3), (3, 2), (3, 0), (3, 3), (1, 1), (1, 3), (0, 3),
)
STRAIGHT = 3
JOINED = CHIPS - STRAIGHT


def offset(t, axis):
    if isinstance(t, int):
        return OWNERS[t][axis]
    return sum(jnp.where(t == i, o[axis], 0) for i, o in enumerate(OWNERS) if o[axis])


def kernel(
    q_hbm, k_hbm, v_hbm, sk_hbm, sv_hbm, len_hbm, out_ref,
    q_ref, len_ref, kbuf, vbuf, vt, s0, s1, sk, sv, qf, qb, qz, qt, osend, oland,
    jsend, jland, dsend, dland, mcols, sfx_o, sfx_b, own_o, own_m,
    load_sem, sib_send, sib_recv, z1_send, z1_recv, q_send, q_recv, o_send, o_recv, z2_send, z2_recv,
):
    p = lax.axis_index("prefix")
    z = lax.axis_index("req")
    core = p % 2
    cx = p // 2 // SIDE
    cy = p // 2 % SIDE
    sibling = p + 1 - 2 * core
    keys = k_hbm.shape[0]
    own_rows = 2 * ZS * GROUP
    far_first = (4, 3, 5, 2, 6, 1, 7)

    def owner(t):
        return (((cx + offset(t, 0)) % SIDE) * SIDE + (cy + offset(t, 1)) % SIDE) * 2 + core

    def worker(t):
        return (((cx + SIDE - offset(t, 0)) % SIDE) * SIDE + (cy + SIDE - offset(t, 1)) % SIDE) * 2 + core

    barrier = pltpu.get_barrier_semaphore()

    def greet(device):
        pl.semaphore_signal(barrier, inc=1, device_id=device, device_id_type=MESH)

    for d in far_first:
        greet((p, (z + d) % ZS))
    for t in sorted(range(1, CHIPS), key=lambda t: -sum(min(a, SIDE - a) for a in OWNERS[t])):
        greet((worker(t), z))
    greet((sibling, z))

    def load(src, dst, i):
        copy = pltpu.make_async_copy(src, dst, load_sem.at[i])
        copy.start()
        return copy

    load_q = load(q_hbm, q_ref, 6)
    load_len = load(len_hbm, len_ref, 7)
    load_v = load(v_hbm, vbuf, 0)
    load_k = load(k_hbm, kbuf.at[0], 1)

    def load_suffix(r):
        return load(sk_hbm.at[r], sk.at[r], 2 + 2 * r), load(sv_hbm.at[r], sv.at[r], 3 + 2 * r)

    loads = [load_suffix(0)]

    load_q.wait()
    own_q = q_ref[...].astype(F32)
    for g in range(KVH):
        for h in range(GROUP):
            at = (g * GROUP + h) * HD
            for r in range(2):
                qf[g, r * GROUP + h : r * GROUP + h + 1, :] = own_q[r : r + 1, at : at + HD]
    for g in range(KVH):
        qb[g] = qf[g].astype(BF16)

    pl.semaphore_wait(barrier, (ZS - 1) + (CHIPS - 1) + 1)

    def z1_copy(d):
        other = (z + d) % ZS
        return pltpu.make_async_remote_copy(
            src_ref=qb.at[other], dst_ref=qz.at[z],
            send_sem=z1_send.at[other], recv_sem=z1_recv.at[z],
            device_id=(p, other), device_id_type=MESH,
        )

    def z1_arrival(d):
        other = (z + d) % ZS
        return pltpu.make_async_remote_copy(
            src_ref=qb.at[other], dst_ref=qz.at[other],
            send_sem=z1_send.at[other], recv_sem=z1_recv.at[other],
            device_id=(p, other), device_id_type=MESH,
        )

    for d in far_first:
        z1_copy(d).start()
    qz[z] = qb[z]

    loads.append(load_suffix(1))
    load_k.wait()
    sib_k = pltpu.make_async_remote_copy(
        src_ref=kbuf.at[0], dst_ref=kbuf.at[1],
        send_sem=sib_send.at[0], recv_sem=sib_recv.at[0],
        device_id=(sibling, z), device_id_type=MESH,
    )
    sib_k.start()
    load_v.wait()
    for c in range(keys // CHUNK):
        part = vbuf[c * CHUNK : (c + 1) * CHUNK, :].astype(F32)
        vt[0, :, c * CHUNK : (c + 1) * CHUNK] = part.T.astype(BF16)
    sib_v = pltpu.make_async_remote_copy(
        src_ref=vt.at[0], dst_ref=vt.at[1],
        send_sem=sib_send.at[1], recv_sem=sib_recv.at[1],
        device_id=(sibling, z), device_id_type=MESH,
    )
    sib_v.start()

    def suffix(r):
        loads[r][0].wait()
        loads[r][1].wait()
        scores = []
        for g in range(KVH):
            q8 = qf[g, r * GROUP : (r + 1) * GROUP, :].astype(BF16)
            scores.append(lax.dot_general(
                q8, sk[r, :, g * HD : (g + 1) * HD], (((1,), (1,)), ((), ())),
                preferred_element_type=F32,
            ))
        s = jnp.concatenate(scores, axis=0)
        live = lax.broadcasted_iota(jnp.int32, s.shape, 1) < len_ref[r]
        s = jnp.where(live, s * LOG2_SCALE, LOW)
        top = jnp.max(s, axis=1, keepdims=True)
        w = jnp.exp2(s - top)
        total = jnp.sum(w, axis=1, keepdims=True)
        mass = jnp.broadcast_to(top + jnp.log2(total), (HEADS, HD))
        share = 1.0 / total
        w = w.astype(BF16)
        for g in range(KVH):
            heads = slice(g * GROUP, (g + 1) * GROUP)
            o = jnp.dot(w[heads], sv[r, :, g * HD : (g + 1) * HD], preferred_element_type=F32)
            sfx_o[g, r * GROUP : (r + 1) * GROUP, :] = o * share[heads]
            sfx_b[g, r * GROUP : (r + 1) * GROUP, :] = mass[heads]

    load_len.wait()
    suffix(0)
    suffix(1)

    for d in far_first:
        z1_arrival(d).wait_recv()
    qt[0] = qz[...].reshape(own_rows, HD).astype(F32).T.astype(BF16)

    def q_copy(t):
        return pltpu.make_async_remote_copy(
            src_ref=qt.at[0], dst_ref=qt.at[t],
            send_sem=q_send.at[t], recv_sem=q_recv.at[t],
            device_id=(worker(t), z), device_id_type=MESH,
        )

    def send_queries(ts):
        for t in ts:
            q_copy(t).start()

    send_queries((1, 2))

    sib_k.wait_recv()
    sib_v.wait_recv()
    per_half = keys // CHUNK

    def split_queries(ts):
        both = jnp.concatenate([qt[t] for t in ts], axis=1).astype(F32) * LOG2_SCALE
        high = both.astype(BF16)
        low = (both - high.astype(F32)).astype(BF16)
        return jnp.concatenate([high, low], axis=0)

    def o_copy(t):
        return pltpu.make_async_remote_copy(
            src_ref=osend.at[t], dst_ref=oland.at[t],
            send_sem=o_send.at[t], recv_sem=o_recv.at[t],
            device_id=(owner(t), z), device_id_type=MESH,
        )

    def z2_copy(k, d):
        other = (z + d) % ZS
        return pltpu.make_async_remote_copy(
            src_ref=dsend.at[k - 1, other] if k else jsend.at[other],
            dst_ref=dland.at[k - 1, z] if k else jland.at[z],
            send_sem=z2_send.at[k, other], recv_sem=z2_recv.at[k, z],
            device_id=(owner(JOINED + k - 1) if k else p, other), device_id_type=MESH,
        )

    def z2_arrival(k, d):
        other = (z + d) % ZS
        return pltpu.make_async_remote_copy(
            src_ref=dsend.at[k - 1, other] if k else jsend.at[other],
            dst_ref=dland.at[k - 1, other] if k else jland.at[other],
            send_sem=z2_send.at[k, other], recv_sem=z2_recv.at[k, other],
            device_id=(owner(JOINED + k - 1) if k else p, other), device_id_type=MESH,
        )

    def others(k):
        return far_first + ((0,) if k else ())

    def pieces(*rows):
        at = lax.broadcasted_iota(jnp.int32, (2 * GROUP, own_rows), 0)
        tile = jnp.zeros((2 * GROUP, own_rows), F32)
        for i, row in enumerate(rows):
            first = row.astype(BF16).astype(F32)
            second = (row - first).astype(BF16).astype(F32)
            for j, piece in enumerate((first, second, row - first - second)):
                tile = jnp.where(at == 3 * i + j, piece, tile)
        return tile.astype(BF16)

    def whole(tile, i):
        tile = tile.astype(F32)
        return tile[3 * i : 3 * i + 1] + tile[3 * i + 1 : 3 * i + 2] + tile[3 * i + 2 : 3 * i + 3]

    def send_straight(k, o, mass):
        o = o.T.reshape(ZS, 2 * GROUP, HD).astype(BF16)
        tile = pieces(mass)
        for other in range(ZS):
            dsend[k - 1, other, : 2 * GROUP, :] = o[other]
            dsend[k - 1, other, 2 * GROUP :, :] = tile
        for d in others(k):
            z2_copy(k, d).start()

    def step(now, later, ts_now, ts_later, top):
        if ts_later:
            cols = len(ts_later) * own_rows
            for t in ts_later:
                if not (isinstance(t, int) and t == 0):
                    q_copy(t).wait_recv()
            queries = split_queries(ts_later)
            new_top = jnp.full((8, cols), LOW, F32)
        if ts_now:
            wide = len(ts_now) * own_rows
            acc = jnp.zeros((HD, wide), F32)
            total = jnp.zeros((8, wide), F32)
        for c in range(2 * per_half):
            half, at = c // per_half, (c % per_half) * CHUNK
            here = slice(c * CHUNK, (c + 1) * CHUNK)
            if ts_later:
                k = kbuf[half, at : at + CHUNK, :]
                s = jnp.dot(jnp.concatenate([k, k], axis=1), queries, preferred_element_type=F32)
                later[here, :cols] = s
                new_top = jnp.maximum(new_top, s.reshape(CHUNK // 8, 8, cols).max(axis=0))
            if ts_now:
                w = jnp.exp2(now[here, :wide] - top)
                total = total + w.reshape(CHUNK // 8, 8, wide).sum(axis=0)
                acc = acc + jnp.dot(vt[half, :, at : at + CHUNK], w.astype(BF16), preferred_element_type=F32)
        if ts_now:
            total = total.sum(axis=0, keepdims=True)
            for u, t in enumerate(ts_now):
                mine = slice(u * own_rows, (u + 1) * own_rows)
                o, part, peak = acc[:, mine], total[:, mine], top[:, mine]
                if isinstance(t, int) and t >= JOINED:
                    send_straight(t - JOINED + 1, o * (1.0 / part), peak + jnp.log2(part))
                elif isinstance(t, int) and t == 0:
                    own_o[...] = o
                    own_m[0] = jnp.broadcast_to(part, (8, own_rows))
                    own_m[1] = jnp.broadcast_to(peak, (8, own_rows))
                else:
                    osend[t, :HD, :] = o.astype(BF16)
                    osend[t, HD:, :] = pieces(part, peak)
                    o_copy(t).start()
        if ts_later:
            return new_top.max(axis=0, keepdims=True)

    def pair(i):
        return (1 + 2 * i, 2 + 2 * i)

    top = step(None, s0, (), (0,), None)
    send_queries((3, 4))
    step(s0, None, (0,), (), top)
    send_queries((5, 6))
    top = step(None, s0, (), pair(0), None)
    send_queries((7, 8))

    def two_steps(j, top):
        @pl.when(j == 0)
        def _():
            send_queries((9, 10))

        @pl.when(j == 1)
        def _():
            send_queries((13, 14))

        top = step(s0, s1, pair(2 * j), pair(2 * j + 1), top)

        @pl.when(j == 0)
        def _():
            send_queries((11, 12))

        @pl.when(j == 1)
        def _():
            send_queries((15,))

        return step(s1, s0, pair(2 * j + 1), pair(2 * j + 2), top)

    rounds = (JOINED - 1) // 4
    top = lax.fori_loop(0, rounds, two_steps, top)
    now, later = s0, s1
    for i in range(2 * rounds, CHIPS // 2 - 1):
        following = pair(i + 1) if i < CHIPS // 2 - 2 else (CHIPS - 1,)
        top = step(now, later, pair(i), following, top)
        now, later = later, now
    step(now, None, (CHIPS - 1,), (), top)

    def join(top, total, out, ts):
        for t in ts:
            o_copy(t).wait_recv()
        sums, tops = [total], [top]
        for t in ts:
            tile = oland[t, HD:, :]
            sums.append(whole(tile, 0))
            tops.append(whole(tile, 1))
        top = functools.reduce(jnp.maximum, tops)
        shares = [jnp.exp2(peak - top) for peak in tops]
        total = sum(part * share for part, share in zip(sums, shares))
        out = out * shares[0]
        for t, share in zip(ts, shares[1:]):
            out = out + oland[t, :HD, :].astype(F32) * share
        return top, total, out

    state = join(own_m[1, 0:1, :], own_m[0, 0:1, :], own_o[...], range(1, JOINED - 2))
    top, total, out = join(*state, range(JOINED - 2, JOINED))
    jsend[:, : 2 * GROUP, :] = (out * (1.0 / total)).T.reshape(ZS, 2 * GROUP, HD)
    jsend[:, 2 * GROUP :, :] = jnp.broadcast_to(top + jnp.log2(total), (ZS, 8, own_rows))
    for d in others(0):
        z2_copy(0, d).start()
    jland[z] = jsend[z]

    kinds = 1 + STRAIGHT
    for k in range(kinds):
        for d in others(k):
            z2_arrival(k, d).wait_recv()
    masses = [jland[g, 2 * GROUP : 2 * GROUP + 1, :] for g in range(KVH)]
    for k in range(STRAIGHT):
        masses += [whole(dland[k, g, 2 * GROUP :, :], 0) for g in range(KVH)]
    mcols[...] = jnp.concatenate(masses, axis=0).T
    mine = mcols[pl.ds(pl.multiple_of(z * 2 * GROUP, 2 * GROUP), 2 * GROUP), :]
    for g in range(KVH):
        masses = [sfx_b[g]]
        for k in range(kinds):
            column = mine[:, k * KVH + g : k * KVH + g + 1]
            masses.append(jnp.broadcast_to(column, (2 * GROUP, HD)))
        outs = [sfx_o[g], jland[g, : 2 * GROUP, :]]
        outs += [dland[k, g, : 2 * GROUP, :].astype(F32) for k in range(STRAIGHT)]
        top = functools.reduce(jnp.maximum, masses)
        shares = [jnp.exp2(m - top) for m in masses]
        joined = sum(o * share for o, share in zip(outs, shares)) / sum(shares)
        for r in range(2):
            for h in range(GROUP):
                at = (g * GROUP + h) * HD
                row = slice(r * GROUP + h, r * GROUP + h + 1)
                out_ref[r : r + 1, at : at + HD] = joined[row, :]

    for d in range(1, ZS):
        z1_copy(d).wait_send()
    for k in range(kinds):
        for d in others(k):
            z2_copy(k, d).wait_send()
    for t in range(1, CHIPS):
        q_copy(t).wait_send()
    for t in range(1, JOINED):
        o_copy(t).wait_send()
    sib_k.wait_send()
    sib_v.wait_send()


def local(queries, prefix_keys, prefix_values, suffix_keys, suffix_values, suffix_lengths):
    keys = prefix_keys.shape[0]
    positions = suffix_keys.shape[1]
    own_rows = 2 * ZS * GROUP
    dma = pltpu.SemaphoreType.DMA
    hbm = pl.BlockSpec(memory_space=pltpu.HBM)
    return pl.pallas_call(
        kernel,
        out_shape=jax.ShapeDtypeStruct((2, HEADS * HD), F32),
        in_specs=[
            hbm, hbm, hbm, hbm, hbm, hbm,
        ],
        out_specs=pl.BlockSpec(memory_space=pltpu.VMEM),
        scratch_shapes=[
            pltpu.VMEM((2, HEADS * HD), BF16),
            pltpu.SMEM((2,), jnp.int32),
            pltpu.VMEM((2, keys, HD), BF16),
            pltpu.VMEM((keys, HD), BF16),
            pltpu.VMEM((2, HD, keys), BF16),
            pltpu.VMEM((2 * keys, 2 * own_rows), F32),
            pltpu.VMEM((2 * keys, 2 * own_rows), F32),
            pltpu.VMEM((2, positions, KVH * HD), BF16),
            pltpu.VMEM((2, positions, KVH * HD), BF16),
            pltpu.VMEM((KVH, 2 * GROUP, HD), F32),
            pltpu.VMEM((KVH, 2 * GROUP, HD), BF16),
            pltpu.VMEM((ZS, 2 * GROUP, HD), BF16),
            pltpu.VMEM((CHIPS, HD, own_rows), BF16),
            pltpu.VMEM((JOINED, HD + 2 * GROUP, own_rows), BF16),
            pltpu.VMEM((JOINED, HD + 2 * GROUP, own_rows), BF16),
            pltpu.VMEM((ZS, 2 * GROUP + 8, HD), F32),
            pltpu.VMEM((KVH, 2 * GROUP + 8, HD), F32),
            pltpu.VMEM((STRAIGHT, ZS, 4 * GROUP, HD), BF16),
            pltpu.VMEM((STRAIGHT, KVH, 4 * GROUP, HD), BF16),
            pltpu.VMEM((own_rows, (1 + STRAIGHT) * KVH), F32),
            pltpu.VMEM((KVH, 2 * GROUP, HD), F32),
            pltpu.VMEM((KVH, 2 * GROUP, HD), F32),
            pltpu.VMEM((HD, own_rows), F32),
            pltpu.VMEM((2, 8, own_rows), F32),
            dma((8,)),
            dma((2,)), dma((2,)),
            dma((ZS,)), dma((ZS,)),
            dma((CHIPS,)), dma((CHIPS,)),
            dma((JOINED,)), dma((JOINED,)),
            dma((1 + STRAIGHT, ZS)), dma((1 + STRAIGHT, ZS)),
        ],
        compiler_params=pltpu.CompilerParams(
            collective_id=0, has_side_effects=True, vmem_limit_bytes=56 * 2**20
        ),
        name="attend",
    )(queries, prefix_keys, prefix_values, suffix_keys, suffix_values, suffix_lengths)


def solution(mesh):
    return jax.shard_map(
        local,
        mesh=mesh,
        in_specs=(
            P(("prefix", "req"), None),
            P("prefix", "req"),
            P("prefix", "req"),
            P(("prefix", "req"), None, None),
            P(("prefix", "req"), None, None),
            P(("prefix", "req")),
        ),
        out_specs=P(("prefix", "req"), None),
        check_vma=False,
    )
```

```python
import functools
import math

import jax
import jax.numpy as jnp
from jax import lax
from jax.experimental import pallas as pl
from jax.experimental.pallas import tpu as pltpu
from jax.sharding import PartitionSpec as P

HEADS = 64
KVH = 8
HD = 128
GROUP = HEADS // KVH
SIDE = 4
CHIPS = SIDE * SIDE
ZS = 8
CHUNK = 1024
MESH = pl.DeviceIdType.MESH
F32 = jnp.float32
BF16 = jnp.bfloat16
LOG2_SCALE = math.log2(math.e) / math.sqrt(HD)
LOW = -1e30
OWNERS = (
    (0, 0), (1, 0), (0, 1), (2, 0), (0, 2), (3, 1), (1, 2), (2, 1),
    (2, 2), (2, 3), (3, 2), (3, 0), (3, 3), (1, 1), (1, 3), (0, 3),
)
STRAIGHT = 3
JOINED = CHIPS - STRAIGHT


def offset(t, axis):
    if isinstance(t, int):
        return OWNERS[t][axis]
    return sum(jnp.where(t == i, o[axis], 0) for i, o in enumerate(OWNERS) if o[axis])


def kernel(
    q_hbm, k_hbm, v_hbm, sk_hbm, sv_hbm, len_hbm, out_ref,
    q_ref, len_ref, kbuf, vbuf, vt, s0, s1, sk, sv, qf, qb, qz, qt, osend, oland,
    jsend, jland, dsend, dland, mcols, sfx_o, sfx_b, own_o, own_m,
    load_sem, sib_send, sib_recv, z1_send, z1_recv, q_send, q_recv, o_send, o_recv, z2_send, z2_recv,
):
    p = lax.axis_index("prefix")
    z = lax.axis_index("req")
    core = p % 2
    cx = p // 2 // SIDE
    cy = p // 2 % SIDE
    sibling = p + 1 - 2 * core
    keys = k_hbm.shape[0]
    own_rows = 2 * ZS * GROUP
    far_first = (4, 3, 5, 2, 6, 1, 7)

    def owner(t):
        return (((cx + offset(t, 0)) % SIDE) * SIDE + (cy + offset(t, 1)) % SIDE) * 2 + core

    def worker(t):
        return (((cx + SIDE - offset(t, 0)) % SIDE) * SIDE + (cy + SIDE - offset(t, 1)) % SIDE) * 2 + core

    barrier = pltpu.get_barrier_semaphore()

    def greet(device):
        pl.semaphore_signal(barrier, inc=1, device_id=device, device_id_type=MESH)

    for d in far_first:
        greet((p, (z + d) % ZS))
    for t in sorted(range(1, CHIPS), key=lambda t: -sum(min(a, SIDE - a) for a in OWNERS[t])):
        greet((worker(t), z))
    greet((sibling, z))

    def load(src, dst, i):
        copy = pltpu.make_async_copy(src, dst, load_sem.at[i])
        copy.start()
        return copy

    load_q = load(q_hbm, q_ref, 6)
    load_len = load(len_hbm, len_ref, 7)
    load_v = load(v_hbm, vbuf, 0)
    load_k = load(k_hbm, kbuf.at[0], 1)

    def load_suffix(r):
        return load(sk_hbm.at[r], sk.at[r], 2 + 2 * r), load(sv_hbm.at[r], sv.at[r], 3 + 2 * r)

    loads = [load_suffix(0)]

    load_q.wait()
    own_q = q_ref[...].astype(F32)
    for g in range(KVH):
        for h in range(GROUP):
            at = (g * GROUP + h) * HD
            for r in range(2):
                qf[g, r * GROUP + h : r * GROUP + h + 1, :] = own_q[r : r + 1, at : at + HD]
    for g in range(KVH):
        qb[g] = qf[g].astype(BF16)

    pl.semaphore_wait(barrier, (ZS - 1) + (CHIPS - 1) + 1)

    def z1_copy(d):
        other = (z + d) % ZS
        return pltpu.make_async_remote_copy(
            src_ref=qb.at[other], dst_ref=qz.at[z],
            send_sem=z1_send.at[other], recv_sem=z1_recv.at[z],
            device_id=(p, other), device_id_type=MESH,
        )

    def z1_arrival(d):
        other = (z + d) % ZS
        return pltpu.make_async_remote_copy(
            src_ref=qb.at[other], dst_ref=qz.at[other],
            send_sem=z1_send.at[other], recv_sem=z1_recv.at[other],
            device_id=(p, other), device_id_type=MESH,
        )

    for d in far_first:
        z1_copy(d).start()
    qz[z] = qb[z]

    loads.append(load_suffix(1))
    load_k.wait()
    sib_k = pltpu.make_async_remote_copy(
        src_ref=kbuf.at[0], dst_ref=kbuf.at[1],
        send_sem=sib_send.at[0], recv_sem=sib_recv.at[0],
        device_id=(sibling, z), device_id_type=MESH,
    )
    sib_k.start()
    load_v.wait()
    for c in range(keys // CHUNK):
        part = vbuf[c * CHUNK : (c + 1) * CHUNK, :].astype(F32)
        vt[0, :, c * CHUNK : (c + 1) * CHUNK] = part.T.astype(BF16)
    sib_v = pltpu.make_async_remote_copy(
        src_ref=vt.at[0], dst_ref=vt.at[1],
        send_sem=sib_send.at[1], recv_sem=sib_recv.at[1],
        device_id=(sibling, z), device_id_type=MESH,
    )
    sib_v.start()

    def suffix(r):
        loads[r][0].wait()
        loads[r][1].wait()
        scores = []
        for g in range(KVH):
            q8 = qf[g, r * GROUP : (r + 1) * GROUP, :].astype(BF16)
            scores.append(lax.dot_general(
                q8, sk[r, :, g * HD : (g + 1) * HD], (((1,), (1,)), ((), ())),
                preferred_element_type=F32,
            ))
        s = jnp.concatenate(scores, axis=0)
        live = lax.broadcasted_iota(jnp.int32, s.shape, 1) < len_ref[r]
        s = jnp.where(live, s * LOG2_SCALE, LOW)
        top = jnp.max(s, axis=1, keepdims=True)
        w = jnp.exp2(s - top)
        total = jnp.sum(w, axis=1, keepdims=True)
        mass = jnp.broadcast_to(top + jnp.log2(total), (HEADS, HD))
        share = 1.0 / total
        w = w.astype(BF16)
        for g in range(KVH):
            heads = slice(g * GROUP, (g + 1) * GROUP)
            o = jnp.dot(w[heads], sv[r, :, g * HD : (g + 1) * HD], preferred_element_type=F32)
            sfx_o[g, r * GROUP : (r + 1) * GROUP, :] = o * share[heads]
            sfx_b[g, r * GROUP : (r + 1) * GROUP, :] = mass[heads]

    load_len.wait()
    suffix(0)
    suffix(1)

    for d in far_first:
        z1_arrival(d).wait_recv()
    qt[0] = qz[...].reshape(own_rows, HD).astype(F32).T.astype(BF16)

    def q_copy(t):
        return pltpu.make_async_remote_copy(
            src_ref=qt.at[0], dst_ref=qt.at[t],
            send_sem=q_send.at[t], recv_sem=q_recv.at[t],
            device_id=(worker(t), z), device_id_type=MESH,
        )

    def send_queries(ts):
        for t in ts:
            q_copy(t).start()

    send_queries((1, 2))

    sib_k.wait_recv()
    sib_v.wait_recv()
    per_half = keys // CHUNK

    def split_queries(ts):
        both = jnp.concatenate([qt[t] for t in ts], axis=1).astype(F32) * LOG2_SCALE
        high = both.astype(BF16)
        low = (both - high.astype(F32)).astype(BF16)
        return jnp.concatenate([high, low], axis=0)

    def o_copy(t):
        return pltpu.make_async_remote_copy(
            src_ref=osend.at[t], dst_ref=oland.at[t],
            send_sem=o_send.at[t], recv_sem=o_recv.at[t],
            device_id=(owner(t), z), device_id_type=MESH,
        )

    def z2_copy(k, d):
        other = (z + d) % ZS
        return pltpu.make_async_remote_copy(
            src_ref=dsend.at[k - 1, other] if k else jsend.at[other],
            dst_ref=dland.at[k - 1, z] if k else jland.at[z],
            send_sem=z2_send.at[k, other], recv_sem=z2_recv.at[k, z],
            device_id=(owner(JOINED + k - 1) if k else p, other), device_id_type=MESH,
        )

    def z2_arrival(k, d):
        other = (z + d) % ZS
        return pltpu.make_async_remote_copy(
            src_ref=dsend.at[k - 1, other] if k else jsend.at[other],
            dst_ref=dland.at[k - 1, other] if k else jland.at[other],
            send_sem=z2_send.at[k, other], recv_sem=z2_recv.at[k, other],
            device_id=(owner(JOINED + k - 1) if k else p, other), device_id_type=MESH,
        )

    def others(k):
        return far_first + ((0,) if k else ())

    def pieces(*rows):
        at = lax.broadcasted_iota(jnp.int32, (2 * GROUP, own_rows), 0)
        tile = jnp.zeros((2 * GROUP, own_rows), F32)
        for i, row in enumerate(rows):
            first = row.astype(BF16).astype(F32)
            second = (row - first).astype(BF16).astype(F32)
            for j, piece in enumerate((first, second, row - first - second)):
                tile = jnp.where(at == 3 * i + j, piece, tile)
        return tile.astype(BF16)

    def whole(tile, i):
        tile = tile.astype(F32)
        return tile[3 * i : 3 * i + 1] + tile[3 * i + 1 : 3 * i + 2] + tile[3 * i + 2 : 3 * i + 3]

    def send_straight(k, o, mass):
        o = o.T.reshape(ZS, 2 * GROUP, HD).astype(BF16)
        tile = pieces(mass)
        for other in range(ZS):
            dsend[k - 1, other, : 2 * GROUP, :] = o[other]
            dsend[k - 1, other, 2 * GROUP :, :] = tile
        for d in others(k):
            z2_copy(k, d).start()

    def step(now, later, ts_now, ts_later, top):
        if ts_later:
            cols = len(ts_later) * own_rows
            for t in ts_later:
                if not (isinstance(t, int) and t == 0):
                    q_copy(t).wait_recv()
            queries = split_queries(ts_later)
            new_top = jnp.full((8, cols), LOW, F32)
        if ts_now:
            wide = len(ts_now) * own_rows
            acc = jnp.zeros((HD, wide), F32)
            total = jnp.zeros((8, wide), F32)
        for c in range(2 * per_half):
            half, at = c // per_half, (c % per_half) * CHUNK
            here = slice(c * CHUNK, (c + 1) * CHUNK)
            if ts_later:
                k = kbuf[half, at : at + CHUNK, :]
                s = jnp.dot(jnp.concatenate([k, k], axis=1), queries, preferred_element_type=F32)
                later[here, :cols] = s
                new_top = jnp.maximum(new_top, s.reshape(CHUNK // 8, 8, cols).max(axis=0))
            if ts_now:
                w = jnp.exp2(now[here, :wide] - top)
                total = total + w.reshape(CHUNK // 8, 8, wide).sum(axis=0)
                acc = acc + jnp.dot(vt[half, :, at : at + CHUNK], w.astype(BF16), preferred_element_type=F32)
        if ts_now:
            total = total.sum(axis=0, keepdims=True)
            for u, t in enumerate(ts_now):
                mine = slice(u * own_rows, (u + 1) * own_rows)
                o, part, peak = acc[:, mine], total[:, mine], top[:, mine]
                if isinstance(t, int) and t >= JOINED:
                    send_straight(t - JOINED + 1, o * (1.0 / part), peak + jnp.log2(part))
                elif isinstance(t, int) and t == 0:
                    own_o[...] = o
                    own_m[0] = jnp.broadcast_to(part, (8, own_rows))
                    own_m[1] = jnp.broadcast_to(peak, (8, own_rows))
                else:
                    osend[t, :HD, :] = o.astype(BF16)
                    osend[t, HD:, :] = pieces(part, peak)
                    o_copy(t).start()
        if ts_later:
            return new_top.max(axis=0, keepdims=True)

    def pair(i):
        return (1 + 2 * i, 2 + 2 * i)

    top = step(None, s0, (), (0,), None)
    send_queries((3, 4))
    step(s0, None, (0,), (), top)
    send_queries((5, 6))
    top = step(None, s0, (), pair(0), None)
    send_queries((7, 8))

    def two_steps(j, top):
        @pl.when(j == 0)
        def _():
            send_queries((9, 10))

        @pl.when(j == 1)
        def _():
            send_queries((13, 14))

        top = step(s0, s1, pair(2 * j), pair(2 * j + 1), top)

        @pl.when(j == 0)
        def _():
            send_queries((11, 12))

        @pl.when(j == 1)
        def _():
            send_queries((15,))

        return step(s1, s0, pair(2 * j + 1), pair(2 * j + 2), top)

    rounds = (JOINED - 1) // 4
    top = lax.fori_loop(0, rounds, two_steps, top)
    now, later = s0, s1
    for i in range(2 * rounds, CHIPS // 2 - 1):
        following = pair(i + 1) if i < CHIPS // 2 - 2 else (CHIPS - 1,)
        top = step(now, later, pair(i), following, top)
        now, later = later, now
    step(now, None, (CHIPS - 1,), (), top)

    def join(top, total, out, ts):
        for t in ts:
            o_copy(t).wait_recv()
        sums, tops = [total], [top]
        for t in ts:
            tile = oland[t, HD:, :]
            sums.append(whole(tile, 0))
            tops.append(whole(tile, 1))
        top = functools.reduce(jnp.maximum, tops)
        shares = [jnp.exp2(peak - top) for peak in tops]
        total = sum(part * share for part, share in zip(sums, shares))
        out = out * shares[0]
        for t, share in zip(ts, shares[1:]):
            out = out + oland[t, :HD, :].astype(F32) * share
        return top, total, out

    state = join(own_m[1, 0:1, :], own_m[0, 0:1, :], own_o[...], range(1, JOINED - 2))
    top, total, out = join(*state, range(JOINED - 2, JOINED))
    jsend[:, : 2 * GROUP, :] = (out * (1.0 / total)).T.reshape(ZS, 2 * GROUP, HD)
    jsend[:, 2 * GROUP :, :] = jnp.broadcast_to(top + jnp.log2(total), (ZS, 8, own_rows))
    for d in others(0):
        z2_copy(0, d).start()
    jland[z] = jsend[z]

    kinds = 1 + STRAIGHT
    for k in range(kinds):
        for d in others(k):
            z2_arrival(k, d).wait_recv()
    masses = [jland[g, 2 * GROUP : 2 * GROUP + 1, :] for g in range(KVH)]
    for k in range(STRAIGHT):
        masses += [whole(dland[k, g, 2 * GROUP :, :], 0) for g in range(KVH)]
    mcols[...] = jnp.concatenate(masses, axis=0).T
    mine = mcols[pl.ds(pl.multiple_of(z * 2 * GROUP, 2 * GROUP), 2 * GROUP), :]
    for g in range(KVH):
        masses = [sfx_b[g]]
        for k in range(kinds):
            column = mine[:, k * KVH + g : k * KVH + g + 1]
            masses.append(jnp.broadcast_to(column, (2 * GROUP, HD)))
        outs = [sfx_o[g], jland[g, : 2 * GROUP, :]]
        outs += [dland[k, g, : 2 * GROUP, :].astype(F32) for k in range(STRAIGHT)]
        top = functools.reduce(jnp.maximum, masses)
        shares = [jnp.exp2(m - top) for m in masses]
        joined = sum(o * share for o, share in zip(outs, shares)) / sum(shares)
        for r in range(2):
            for h in range(GROUP):
                at = (g * GROUP + h) * HD
                row = slice(r * GROUP + h, r * GROUP + h + 1)
                out_ref[r : r + 1, at : at + HD] = joined[row, :]

    for d in range(1, ZS):
        z1_copy(d).wait_send()
    for k in range(kinds):
        for d in others(k):
            z2_copy(k, d).wait_send()
    for t in range(1, CHIPS):
        q_copy(t).wait_send()
    for t in range(1, JOINED):
        o_copy(t).wait_send()
    sib_k.wait_send()
    sib_v.wait_send()


def local(queries, prefix_keys, prefix_values, suffix_keys, suffix_values, suffix_lengths):
    keys = prefix_keys.shape[0]
    positions = suffix_keys.shape[1]
    own_rows = 2 * ZS * GROUP
    dma = pltpu.SemaphoreType.DMA
    hbm = pl.BlockSpec(memory_space=pltpu.HBM)
    return pl.pallas_call(
        kernel,
        out_shape=jax.ShapeDtypeStruct((2, HEADS * HD), F32),
        in_specs=[
            hbm, hbm, hbm, hbm, hbm, hbm,
        ],
        out_specs=pl.BlockSpec(memory_space=pltpu.VMEM),
        scratch_shapes=[
            pltpu.VMEM((2, HEADS * HD), BF16),
            pltpu.SMEM((2,), jnp.int32),
            pltpu.VMEM((2, keys, HD), BF16),
            pltpu.VMEM((keys, HD), BF16),
            pltpu.VMEM((2, HD, keys), BF16),
            pltpu.VMEM((2 * keys, 2 * own_rows), F32),
            pltpu.VMEM((2 * keys, 2 * own_rows), F32),
            pltpu.VMEM((2, positions, KVH * HD), BF16),
            pltpu.VMEM((2, positions, KVH * HD), BF16),
            pltpu.VMEM((KVH, 2 * GROUP, HD), F32),
            pltpu.VMEM((KVH, 2 * GROUP, HD), BF16),
            pltpu.VMEM((ZS, 2 * GROUP, HD), BF16),
            pltpu.VMEM((CHIPS, HD, own_rows), BF16),
            pltpu.VMEM((JOINED, HD + 2 * GROUP, own_rows), BF16),
            pltpu.VMEM((JOINED, HD + 2 * GROUP, own_rows), BF16),
            pltpu.VMEM((ZS, 2 * GROUP + 8, HD), F32),
            pltpu.VMEM((KVH, 2 * GROUP + 8, HD), F32),
            pltpu.VMEM((STRAIGHT, ZS, 4 * GROUP, HD), BF16),
            pltpu.VMEM((STRAIGHT, KVH, 4 * GROUP, HD), BF16),
            pltpu.VMEM((own_rows, (1 + STRAIGHT) * KVH), F32),
            pltpu.VMEM((KVH, 2 * GROUP, HD), F32),
            pltpu.VMEM((KVH, 2 * GROUP, HD), F32),
            pltpu.VMEM((HD, own_rows), F32),
            pltpu.VMEM((2, 8, own_rows), F32),
            dma((8,)),
            dma((2,)), dma((2,)),
            dma((ZS,)), dma((ZS,)),
            dma((CHIPS,)), dma((CHIPS,)),
            dma((JOINED,)), dma((JOINED,)),
            dma((1 + STRAIGHT, ZS)), dma((1 + STRAIGHT, ZS)),
        ],
        compiler_params=pltpu.CompilerParams(
            collective_id=0, has_side_effects=True, vmem_limit_bytes=107 * 2**19
        ),
        name="attend",
    )(queries, prefix_keys, prefix_values, suffix_keys, suffix_values, suffix_lengths)


def solution(mesh):
    return jax.shard_map(
        local,
        mesh=mesh,
        in_specs=(
            P(("prefix", "req"), None),
            P("prefix", "req"),
            P("prefix", "req"),
            P(("prefix", "req"), None, None),
            P(("prefix", "req"), None, None),
            P(("prefix", "req")),
        ),
        out_specs=P(("prefix", "req"), None),
        check_vma=False,
    )
```
